32 devices in a mesh: groups: 1, frames: 32 (over z, y, x, core).
Axes of the slice: x: 2, y: 2, z: 4, core: 2. Of those that a mesh axis runs over, the one named last changes fastest.
Arguments:
- features: bfloat16 [32, 4096, 256], P(('groups', 'frames')), may hold values from -6 to 6
- query_frame: int32 [128], P('groups'), may hold values from 0 to 31
- query_pos: int32 [128], P('groups'), may hold values from 0 to 4095
- frame_order: int32 [32], P('groups'), may hold values from 0 to 31, each once
- conv1_weight: float32 [16, 9], replicated, may hold values from -2 to 2
- conv1_bias: float32 [16], replicated, may hold values from -0.5 to 0.5
- conv2_weight: bfloat16 [32, 16, 2, 2], replicated, may hold values from -0.75 to 0.75
- proj_weight: bfloat16 [2048, 512], replicated, may hold values from -0.125 to 0.125
- norm_gains: float32 [2, 2, 512], replicated, may hold values from 0.25 to 1.75
- time_kernels: float32 [2, 3, 512], replicated, may hold values from -3 to 3
- mix_up: bfloat16 [2, 512, 2048], replicated, may hold values from -0.25 to 0.25
- mix_down: bfloat16 [2, 2048, 512], replicated, may hold values from -0.125 to 0.125
Outputs:
- mixed: bfloat16 [32, 128, 512], P(('groups', 'frames'))
The draws below stay inside these ranges and needn't reach their ends.
Inputs may be any that keep to these rules, and one draw needn't show every extreme that they name: query_pos = y * 64 + x. `frame_order`: a permutation: every time index once.
All inputs are finite; a program needn't handle non-finite values.
Results may differ from the reference program's by a relative error of at most 0.015.
Values may be sent and summed in bfloat16 or wider, within the bound.
No kernel may reach another device: no remote copies, remote signals or barrier semaphores. Data moves between devices by JAX's collectives and lax.ppermute only.
A program may use at most 128 MiB of HBM per device.

```python
import jax
import jax.numpy as jnp
from jax import lax

MAP = 64
C = 256
CH1 = 16
CH2 = 32
GRID = 8
P_SIZE = 512
HID = 2048
BLOCKS = 2
FRAMES = 32
TRACKS = 128


def place_ends(result, own_key, least, top_value):
    shape = result.shape
    place = [jax.random.randint(jax.random.fold_in(own_key, axis), (), 0, shape[axis]) for axis in range(len(shape))]
    result = result.at[tuple(place)].set(least)
    longest = shape.index(max(shape))
    place[longest] = (place[longest] + 1) % shape[longest]
    return result.at[tuple(place)].set(top_value)


def block_scale(key, extent, cuts, low, high):
    def one(dim, shards_of):
        draws = jax.random.uniform(jax.random.fold_in(jax.random.fold_in(key, 6), dim), (shards_of,), jnp.float32, low / len(cuts), high / len(cuts))
        return jnp.repeat(jnp.exp(draws), extent[dim] // shards_of).reshape((-1,) + (1,) * (len(extent) - dim - 1))

    loudness = one(*cuts[0])
    for cut in cuts[1:]:
        loudness = loudness * one(*cut)
    return loudness


def normal_values(rng, dims, deviation, limit, pieces=(), kind=jnp.bfloat16):
    result = jax.random.normal(rng, dims, jnp.float32) * deviation
    if len(pieces) > 0:
        result = block_scale(rng, dims, pieces, -0.22, 0.18) * result
    return jnp.clip(result, min=-limit, max=limit).astype(kind)


def setup_inputs(seed: int = 0, part: int = 0) -> dict:
    key_list = jax.random.split(jax.random.key(seed), 13)
    own_keys = jax.random.split(jax.random.fold_in(key_list[12], part), 13)
    return {
        "features": normal_values(own_keys[0], (FRAMES, MAP * MAP, C), 1.0, 6.0, ((0, 32),)),
        "query_frame": place_ends(jax.random.randint(own_keys[1], (TRACKS,), 0, FRAMES), jax.random.fold_in(own_keys[1], 1), 0, FRAMES - 1).astype(jnp.int32),
        "query_pos": place_ends(jax.random.randint(own_keys[2], (TRACKS,), 0, MAP * MAP), jax.random.fold_in(own_keys[2], 1), 0, (MAP * MAP) - 1).astype(jnp.int32),
        "frame_order": jax.random.permutation(own_keys[3], FRAMES).astype(jnp.int32),
        "conv1_weight": normal_values(key_list[4], (CH1, 9), 9 ** -0.5, 2.0, (), jnp.float32),
        "conv1_bias": jnp.clip(jax.random.uniform(key_list[5], (CH1,), jnp.float32, -0.5, 0.5), -0.5, 0.5),
        "conv2_weight": normal_values(key_list[6], (CH2, CH1, 2, 2), (CH1 * 4) ** -0.5, 0.75),
        "proj_weight": normal_values(key_list[7], (CH2 * GRID * GRID, P_SIZE), (CH2 * GRID * GRID) ** -0.5, 0.125),
        "norm_gains": jnp.clip(1.0 + 0.15 * jax.random.normal(key_list[8], (BLOCKS, 2, P_SIZE), jnp.float32), 0.25, 1.75),
        "time_kernels": normal_values(key_list[9], (BLOCKS, 3, P_SIZE), 0.5, 3.0, (), jnp.float32),
        "mix_up": normal_values(key_list[10], (BLOCKS, P_SIZE, HID), P_SIZE ** -0.5, 0.25),
        "mix_down": normal_values(key_list[11], (BLOCKS, HID, P_SIZE), HID ** -0.5, 0.125),
    }


def layer_norm(values):
    center = values - lax.optimization_barrier(jnp.mean(values, axis=-1, keepdims=True))
    spread = lax.optimization_barrier(jnp.mean(center * center, axis=-1, keepdims=True))
    return center * lax.rsqrt(spread + 1e-05)

def frame_rows(feature_map, queries, conv1_weight, conv1_bias, conv2_weight, proj_weight):
    channels = feature_map.shape[1]
    count = queries.shape[0]
    corr = jnp.dot(feature_map, queries.T, preferred_element_type=jnp.float32) / jnp.sqrt(jnp.float32(channels))
    cube = corr.reshape(MAP, MAP, count)
    padded = jnp.pad(cube, ((1, 1), (1, 1), (0, 0)))
    total = jnp.zeros((CH1, MAP, MAP, count), jnp.float32) + conv1_bias[:, None, None, None]
    for shift_y in range(3):
        for shift_x in range(3):
            window = padded[shift_y:shift_y + MAP, shift_x:shift_x + MAP, :]
            total = total + conv1_weight[:, 3 * shift_y + shift_x][:, None, None, None] * window[None]
    first = jax.nn.relu(total).astype(jnp.bfloat16)
    half = MAP // 2
    blocks = first.reshape(CH1, half, 2, half, 2, count).astype(jnp.float32)
    second = jnp.einsum('cyaxbt,ocab->oyxt', blocks, conv2_weight.astype(jnp.float32))
    second = jax.nn.relu(second)
    width = half // GRID
    pooled = second.reshape(CH2, GRID, width, GRID, width, count).mean(axis=(2, 4))
    pooled = pooled.reshape(CH2 * GRID * GRID, count).astype(jnp.bfloat16)
    rows = lax.dot_general(pooled, proj_weight, (((0,), (0,)), ((), ())), preferred_element_type=jnp.float32)
    return rows.astype(jnp.bfloat16)

def mix_tracks(rows, frame_order, norm_gains, time_kernels, mix_up, mix_down):
    total_frames = rows.shape[0]
    inverse = jnp.zeros((total_frames,), jnp.int32).at[frame_order].set(jnp.arange(total_frames, dtype=jnp.int32))
    state = rows[inverse].astype(jnp.float32)
    width = state.shape[-1]
    for block in range(norm_gains.shape[0]):
        normed = layer_norm(state) * norm_gains[block, 0]
        padded = jnp.pad(normed, ((1, 1), (0, 0), (0, 0)))
        state = state + time_kernels[block, 0] * padded[:-2] + time_kernels[block, 1] * padded[1:-1] + time_kernels[block, 2] * padded[2:]
        inner = (layer_norm(state) * norm_gains[block, 1]).astype(jnp.bfloat16).reshape(-1, width)
        hidden = jax.nn.gelu(jnp.dot(inner, mix_up[block], preferred_element_type=jnp.float32)).astype(jnp.bfloat16)
        state = state + jnp.dot(hidden, mix_down[block], preferred_element_type=jnp.float32).reshape(state.shape)
    return state[frame_order].astype(jnp.bfloat16)

def reference(features, query_frame, query_pos, frame_order, conv1_weight, conv1_bias, conv2_weight, proj_weight, norm_gains, time_kernels, mix_up, mix_down):
    queries = features[query_frame, query_pos]

    def one_frame(feature_map):
        return frame_rows(feature_map, queries, conv1_weight, conv1_bias, conv2_weight, proj_weight)
    rows = lax.map(one_frame, features)
    return mix_tracks(rows, frame_order, norm_gains, time_kernels, mix_up, mix_down)
```

```python
import math

import jax
import jax.numpy as jnp
from jax import lax
from jax.experimental import pallas as pl
from jax.experimental.pallas import tpu as pltpu
from jax.sharding import PartitionSpec as P

AXIS = "frames"
NT = (((1,), (1,)), ((), ()))
TN = (((0,), (0,)), ((), ()))


def sum_over_frames(values, devices):
    if devices & (devices - 1):
        return lax.psum(values, AXIS)
    bit = 1
    while bit < devices:
        if bit == 1 or 2 * bit >= devices:
            shifts = (bit,)
        else:
            shifts = (bit, 2 * bit, 3 * bit)
        arrived = [
            lax.ppermute(values, AXIS, [(i, i ^ shift) for i in range(devices)])
            for shift in shifts
        ]
        for part in arrived:
            values = values + part
        bit *= len(shifts) + 1
    return values


def conv_tables(conv1_weight, conv1_bias, conv2_weight, proj_weight, side, grid):
    ch1 = conv1_weight.shape[0]
    ch2 = conv2_weight.shape[0]
    width = side // 2 // grid
    group = max(1, min(grid, 256 // (4 * ch1)))
    lanes = jnp.arange(width * grid * ch1 * 4, dtype=jnp.int32)
    col_b = lanes % 2
    row_a = (lanes // 2) % 2
    chan = (lanes // 4) % ch1
    grid_j = (lanes // (4 * ch1)) % grid
    win_s = lanes // (4 * ch1 * grid)
    at_x = 2 * (grid_j * width + win_s) + col_b
    positions = jnp.arange(4 * side, dtype=jnp.int32)
    diff = (positions // side * (4 * side) + positions % side)[:, None] - (
        row_a * (4 * side) + at_x - 1
    )[None, :]
    taps = conv1_weight.astype(jnp.bfloat16).T
    taps = jnp.broadcast_to(taps[:, None, :, None], (9, width * grid, ch1, 4)).reshape(9, -1)
    first = jnp.zeros(diff.shape, jnp.bfloat16)
    for dy in range(3):
        for dx in range(3):
            first = jnp.where(diff == dy * (4 * side) + dx, taps[3 * dy + dx][None, :], first)
    bias = jnp.broadcast_to(conv1_bias[None, :, None], (group, ch1, 4)).reshape(1, -1)
    small = conv2_weight.reshape(ch2, ch1 * 4).T
    eye = jnp.eye(group, dtype=small.dtype)
    second = (eye[:, None, :, None] * small[None, :, None, :]).reshape(
        group * ch1 * 4, group * ch2
    )
    proj = proj_weight.reshape(ch2, grid * grid, -1).transpose(1, 0, 2)
    return first, bias, second, proj.reshape(proj_weight.shape)


def rows_kernel(
    side, grid, query_ref, feat_hbm, first_ref, bias_ref, second_ref, proj_ref, out_ref,
    feat, windows, sems,
):
    half = side // 2
    width = half // grid
    count, channels = query_ref.shape
    points = side * side
    pieces = sems.shape[0]
    piece = points // pieces
    copies = [
        pltpu.make_async_copy(
            feat_hbm.at[0, pl.ds(n * piece, piece)],
            feat.at[pl.ds(side + n * piece, piece)],
            sems.at[n],
        )
        for n in range(pieces)
    ]
    for copy in copies:
        copy.start()
    edge = jnp.zeros((side, channels), feat.dtype)
    feat[pl.ds(0, side)] = edge
    feat[pl.ds(side + points, side)] = edge
    query = query_ref[...]
    scale = 1.0 / math.sqrt(channels)
    step = 2 * side
    ready = 0
    for t in range(half + 1):
        while ready < pieces and (t + 1) * step > side + ready * piece:
            copies[ready].wait()
            ready += 1
        part = lax.dot_general(
            query, feat[t * step : (t + 1) * step], NT, preferred_element_type=jnp.float32
        )
        part = (part * scale).astype(jnp.bfloat16)
        if t < half:
            windows[t, :, :step] = part
        if t > 0:
            windows[t - 1, :, step:] = part
    bias = bias_ref[...]
    second = second_ref[...]
    lanes_in, lanes_out = second.shape
    groups = first_ref.shape[1] // (width * lanes_in)

    def grid_row(i, total):
        window = windows[pl.ds(i * width, width)].reshape(width * count, 2 * step)
        sums = [None] * groups
        for s in range(width):
            for g in range(groups):
                n = s * groups + g
                one = jnp.dot(
                    window,
                    first_ref[:, n * lanes_in : (n + 1) * lanes_in],
                    preferred_element_type=jnp.float32,
                )
                one = jnp.maximum(one + bias, 0.0).astype(jnp.bfloat16)
                two = jnp.dot(one, second, preferred_element_type=jnp.float32)
                two = jnp.maximum(two, 0.0)
                for u in range(width):
                    term = two[u * count : (u + 1) * count]
                    sums[g] = term if sums[g] is None else sums[g] + term
        pooled = jnp.concatenate(sums, axis=1) * (1.0 / (width * width))
        size = groups * lanes_out
        weights = proj_ref[pl.ds(pl.multiple_of(i * size, size), size)]
        return total + jnp.dot(
            pooled.astype(jnp.bfloat16), weights, preferred_element_type=jnp.float32
        )

    total = lax.fori_loop(
        0, grid, grid_row, jnp.zeros((count, out_ref.shape[1]), jnp.float32)
    )
    out_ref[...] = total.astype(out_ref.dtype)


def frame_rows(features, queries, conv1_weight, conv1_bias, conv2_weight, proj_weight):
    points, channels = features.shape[1:]
    count = queries.shape[0]
    side = math.isqrt(points)
    grid = math.isqrt(proj_weight.shape[0] // conv2_weight.shape[0])
    first, bias, second, proj = conv_tables(
        conv1_weight, conv1_bias, conv2_weight, proj_weight, side, grid
    )
    vmem = pl.BlockSpec(memory_space=pltpu.VMEM)

    def kernel(*refs):
        rows_kernel(side, grid, *refs)

    return pl.pallas_call(
        kernel,
        out_shape=jax.ShapeDtypeStruct((count, proj.shape[1]), jnp.bfloat16),
        in_specs=[vmem, pl.BlockSpec(memory_space=pl.ANY), vmem, vmem, vmem, vmem],
        out_specs=vmem,
        scratch_shapes=[
            pltpu.VMEM((points + 2 * side, channels), jnp.bfloat16),
            pltpu.VMEM((side // 2, count, 4 * side), jnp.bfloat16),
            pltpu.SemaphoreType.DMA((4,)),
        ],
        compiler_params=pltpu.CompilerParams(vmem_limit_bytes=32 * 1024 * 1024),
        name="frame_rows",
    )(queries, features, first, bias, second, proj)


def layer_norm(values):
    center = values - jnp.mean(values, axis=-1, keepdims=True)
    spread = jnp.mean(center * center, axis=-1, keepdims=True)
    return center * lax.rsqrt(spread + 1e-05)


def mixer_kernel(tracks, rows_ref, place_ref, gain_ref, time_ref, up_ref, down_ref, out_ref):
    length = rows_ref.shape[0]
    slots = lax.broadcasted_iota(jnp.int32, (length, length), 0)
    order = (slots == place_ref[...]).astype(jnp.bfloat16)
    state = jnp.dot(order, rows_ref[...], preferred_element_type=jnp.float32)
    edge = jnp.zeros((tracks, state.shape[1]), jnp.float32)
    hidden_size = up_ref.shape[2]
    chunk = min(512, hidden_size)
    for block in range(up_ref.shape[0]):
        normed = layer_norm(state) * gain_ref[block, 0:1]
        before = jnp.concatenate([edge, normed[:-tracks]], axis=0)
        after = jnp.concatenate([normed[tracks:], edge], axis=0)
        state = (
            state
            + time_ref[block, 0:1] * before
            + time_ref[block, 1:2] * normed
            + time_ref[block, 2:3] * after
        )
        inner = (layer_norm(state) * gain_ref[block, 1:2]).astype(jnp.bfloat16)
        for c in range(0, hidden_size, chunk):
            hidden = jnp.dot(
                inner, up_ref[block, :, c : c + chunk], preferred_element_type=jnp.float32
            )
            hidden = jax.nn.gelu(hidden, approximate=True).astype(jnp.bfloat16)
            state = state + jnp.dot(
                hidden, down_ref[block, c : c + chunk, :], preferred_element_type=jnp.float32
            )
    out_ref[...] = lax.dot_general(
        order, state.astype(jnp.bfloat16), TN, preferred_element_type=jnp.float32
    ).astype(out_ref.dtype)


def mix_tracks(rows, frame_order, norm_gains, time_kernels, mix_up, mix_down, tracks):
    place = (frame_order[:, None] * tracks + jnp.arange(tracks, dtype=jnp.int32)).reshape(1, -1)
    vmem = pl.BlockSpec(memory_space=pltpu.VMEM)

    def kernel(*refs):
        mixer_kernel(tracks, *refs)

    return pl.pallas_call(
        kernel,
        out_shape=jax.ShapeDtypeStruct(rows.shape, rows.dtype),
        in_specs=[vmem] * 6,
        out_specs=vmem,
        compiler_params=pltpu.CompilerParams(vmem_limit_bytes=32 * 1024 * 1024),
        name="mixer",
    )(rows, place, norm_gains, time_kernels, mix_up, mix_down)


def on_device(
    features,
    query_frame,
    query_pos,
    frame_order,
    conv1_weight,
    conv1_bias,
    conv2_weight,
    proj_weight,
    norm_gains,
    time_kernels,
    mix_up,
    mix_down,
):
    devices = lax.axis_size(AXIS)
    track_count = query_frame.shape[0]
    per_device = track_count // devices
    owned = query_frame == lax.axis_index(AXIS)
    picked = jnp.where(owned[:, None], features[0, query_pos], jnp.bfloat16(0.0))
    queries = sum_over_frames(picked, devices)
    rows = frame_rows(features, queries, conv1_weight, conv1_bias, conv2_weight, proj_weight)
    rows = lax.all_to_all(rows, AXIS, split_axis=0, concat_axis=0, tiled=True)
    mixed = mix_tracks(
        rows, frame_order, norm_gains, time_kernels, mix_up, mix_down, per_device
    )
    mixed = lax.all_to_all(mixed, AXIS, split_axis=0, concat_axis=0, tiled=True)
    return mixed[None]


def solution(mesh):
    placed = (
        P(("groups", "frames"), None, None),
        P("groups"),
        P("groups"),
        P("groups"),
        P(),
        P(),
        P(),
        P(),
        P(),
        P(),
        P(),
        P(),
    )
    return jax.shard_map(
        on_device,
        mesh=mesh,
        in_specs=placed,
        out_specs=P(("groups", "frames"), None, None),
        check_vma=False,
    )
```

```python
import math

import jax
import jax.numpy as jnp
from jax import lax
from jax.experimental import pallas as pl
from jax.experimental.pallas import tpu as pltpu
from jax.sharding import PartitionSpec as P

AXIS = "frames"
NT = (((1,), (1,)), ((), ()))
TN = (((0,), (0,)), ((), ()))
VMEM = pl.BlockSpec(memory_space=pltpu.VMEM)
HBM = pl.BlockSpec(memory_space=pltpu.HBM)
MIB = 1024 * 1024


def iota(shape, axis):
    return lax.broadcasted_iota(jnp.int32, shape, axis)


def exchange_stages(devices):
    stages = []
    bit = 1
    while bit < devices:
        if bit == 1 or 2 * bit >= devices:
            stages.append((bit,))
        else:
            stages.append((bit, 2 * bit, 3 * bit))
        bit *= len(stages[-1]) + 1
    return stages


def exchange(values, shifts, devices):
    arrived = [
        lax.ppermute(values, AXIS, [(i, i ^ shift) for i in range(devices)]) for shift in shifts
    ]
    for part in arrived:
        values = values + part
    return values


def pick_kernel(pieces, wanted_ref, feat_hbm, out_ref, feat, sems):
    points, channels = feat.shape
    count = wanted_ref.shape[1]
    piece = points // pieces
    copies = [
        pltpu.make_async_copy(
            feat_hbm.at[0, pl.ds(n * piece, piece)], feat.at[pl.ds(n * piece, piece)], sems.at[n]
        )
        for n in range(pieces)
    ]
    for copy in copies:
        copy.start()
    wanted = jnp.broadcast_to(wanted_ref[...], (count, count)).T
    total = jnp.zeros((count, channels), jnp.float32)
    for n in range(pieces):
        parts = []
        for at in range(n * piece, (n + 1) * piece, count):
            parts.append((wanted == iota((count, count), 1) + at).astype(jnp.bfloat16))
        hot = jnp.concatenate(parts, axis=1)
        copies[n].wait()
        total = total + jnp.dot(
            hot, feat[n * piece : (n + 1) * piece], preferred_element_type=jnp.float32
        )
    out_ref[...] = total.astype(out_ref.dtype)


def pick_queries(features, query_frame, query_pos):
    points, channels = features.shape[1:]
    count = query_frame.shape[0]
    wanted = jnp.where(query_frame == lax.axis_index(AXIS), query_pos, -1)
    pieces = 4

    def kernel(*refs):
        pick_kernel(pieces, *refs)

    return pl.pallas_call(
        kernel,
        out_shape=jax.ShapeDtypeStruct((count, channels), features.dtype),
        in_specs=[VMEM, HBM],
        out_specs=VMEM,
        scratch_shapes=[
            pltpu.VMEM((points, channels), features.dtype),
            pltpu.SemaphoreType.DMA((pieces,)),
        ],
        compiler_params=pltpu.CompilerParams(vmem_limit_bytes=53 * MIB),
        name="pick_queries",
    )(wanted.reshape(1, -1), features)


def tables_kernel(
    side, grid, taps_ref, bias_ref, small_ref, first_ref, lane_bias_ref, second_ref
):
    ch1, ch2 = taps_ref.shape[0], small_ref.shape[1]
    width = side // 2 // grid
    lanes = grid * ch1 * 4
    rows = 4 * side
    lane = iota((1, lanes), 1)
    hot = (iota((ch1, lanes), 0) == iota((ch1, lanes), 1) // 4 % ch1).astype(jnp.float32)
    lane_bias_ref[...] = jnp.dot(
        bias_ref[...], hot, precision=lax.Precision.HIGHEST, preferred_element_type=jnp.float32
    )
    taps = lax.dot_general(
        taps_ref[...].astype(jnp.bfloat16),
        hot.astype(jnp.bfloat16),
        TN,
        preferred_element_type=jnp.float32,
    )
    at = lane // 2 % 2 * rows + 2 * width * (lane // (4 * ch1)) + lane % 2 - 1
    spot = iota((rows, 1), 0)
    diff = spot // side * rows + spot % side - at
    for s in range(width):
        first = jnp.zeros((rows, lanes), jnp.float32)
        for dy in range(3):
            for dx in range(3):
                n = 3 * dy + dx
                first = jnp.where(diff == dy * rows + dx + 2 * s, taps[n : n + 1], first)
        first_ref[:, s * lanes : (s + 1) * lanes] = first.astype(jnp.bfloat16)

    out_lanes = ch2 * grid
    hot = (iota((ch2, out_lanes), 0) == iota((ch2, out_lanes), 1) // grid).astype(jnp.bfloat16)
    wide = jnp.dot(small_ref[...], hot, preferred_element_type=jnp.float32)
    for j in range(grid):
        second_ref[j * 4 * ch1 : (j + 1) * 4 * ch1] = jnp.where(
            iota(wide.shape, 1) % grid == j, wide, 0.0
        ).astype(jnp.bfloat16)


def conv_tables(conv1_weight, conv1_bias, conv2_weight, side, grid):
    ch1 = conv1_weight.shape[0]
    ch2 = conv2_weight.shape[0]
    lanes = grid * ch1 * 4

    def kernel(*refs):
        tables_kernel(side, grid, *refs)

    return pl.pallas_call(
        kernel,
        out_shape=[
            jax.ShapeDtypeStruct((4 * side, side // 2 // grid * lanes), jnp.bfloat16),
            jax.ShapeDtypeStruct((1, lanes), jnp.float32),
            jax.ShapeDtypeStruct((lanes, ch2 * grid), jnp.bfloat16),
        ],
        in_specs=[VMEM] * 3,
        out_specs=[VMEM] * 3,
        compiler_params=pltpu.CompilerParams(vmem_limit_bytes=24 * MIB),
        name="conv_tables",
    )(conv1_weight, conv1_bias.reshape(1, ch1), conv2_weight.transpose(1, 2, 3, 0).reshape(ch1 * 4, ch2))


def rows_kernel(
    side, grid, query_ref, feat_ref, first_ref, bias_ref, second_ref, proj_ref, out_ref, windows, sums
):
    half = side // 2
    width = half // grid
    count, channels = query_ref.shape
    query = query_ref[...]
    scale = 1.0 / math.sqrt(channels)
    step = 2 * side
    for t in range(half + 1):
        part = lax.dot_general(
            query, feat_ref[t * step : (t + 1) * step], NT, preferred_element_type=jnp.float32
        )
        part = (part * scale).astype(jnp.bfloat16)
        if t < half:
            windows[t, :, :step] = part
        if t > 0:
            windows[t - 1, :, step:] = part
    bias = bias_ref[...]
    lanes_in, lanes_out = second_ref.shape
    for s in range(width):
        for i in range(grid):
            window = windows[i * width : (i + 1) * width].reshape(width * count, 2 * step)
            one = jnp.dot(
                window,
                first_ref[:, s * lanes_in : (s + 1) * lanes_in],
                preferred_element_type=jnp.float32,
            )
            one = jnp.maximum(one + bias, 0.0).astype(jnp.bfloat16)
            two = jnp.dot(one, second_ref[...], preferred_element_type=jnp.float32)
            two = jnp.maximum(two, 0.0).reshape(width, count, lanes_out)
            summed = two[0]
            for u in range(1, width):
                summed = summed + two[u]
            sums[i] = summed if s == 0 else sums[i] + summed
    total = jnp.zeros(out_ref.shape, jnp.float32)
    for i in range(grid):
        pooled = (sums[i] * (1.0 / (width * width))).astype(jnp.bfloat16)
        total = total + jnp.dot(
            pooled,
            proj_ref[i * lanes_out : (i + 1) * lanes_out],
            preferred_element_type=jnp.float32,
        )
    out_ref[...] = total.astype(out_ref.dtype)


def frame_rows(queries, padded, tables, proj, side, grid):
    count = queries.shape[0]

    def kernel(*refs):
        rows_kernel(side, grid, *refs)

    return pl.pallas_call(
        kernel,
        out_shape=jax.ShapeDtypeStruct((count, proj.shape[1]), jnp.bfloat16),
        in_specs=[VMEM] * 6,
        out_specs=VMEM,
        scratch_shapes=[
            pltpu.VMEM((side // 2, count, 4 * side), jnp.bfloat16),
            pltpu.VMEM((grid, count, proj.shape[0] // grid), jnp.float32),
        ],
        compiler_params=pltpu.CompilerParams(vmem_limit_bytes=32 * MIB),
        name="frame_rows",
    )(queries, padded, *tables, proj)


def layer_norm(values):
    center = values - jnp.mean(values, axis=-1, keepdims=True)
    spread = jnp.mean(center * center, axis=-1, keepdims=True)
    return center * lax.rsqrt(spread + 1e-05)


def mixer_kernel(
    tracks, rows_ref, place_ref, gain_ref, time_ref, up_hbm, down_hbm, out_ref, up_ref, down_ref, sems
):
    blocks, width, hidden_size = up_hbm.shape
    chunk = min(512, hidden_size)
    starts = range(0, hidden_size, chunk)
    ups, downs = {}, {}
    for block in range(blocks):
        for n, c in enumerate(starts):
            at = (block, slice(None), pl.ds(c, chunk))
            ups[block, n] = pltpu.make_async_copy(
                up_hbm.at[at], up_ref.at[at], sems.at[0, block, n]
            )
            ups[block, n].start()
        for n, c in enumerate(starts):
            at = (block, pl.ds(c, chunk))
            downs[block, n] = pltpu.make_async_copy(
                down_hbm.at[at], down_ref.at[at], sems.at[1, block, n]
            )
            downs[block, n].start()
    length = rows_ref.shape[0]
    slots = iota((length, length), 0)
    order = (slots == place_ref[...]).astype(jnp.bfloat16)
    state = jnp.dot(order, rows_ref[...], preferred_element_type=jnp.float32)
    edge = jnp.zeros((tracks, width), jnp.float32)
    for block in range(blocks):
        normed = layer_norm(state) * gain_ref[block, 0:1]
        before = jnp.concatenate([edge, normed[:-tracks]], axis=0)
        after = jnp.concatenate([normed[tracks:], edge], axis=0)
        state = (
            state
            + time_ref[block, 0:1] * before
            + time_ref[block, 1:2] * normed
            + time_ref[block, 2:3] * after
        )
        inner = (layer_norm(state) * gain_ref[block, 1:2]).astype(jnp.bfloat16)
        parts = []
        for n, c in enumerate(starts):
            ups[block, n].wait()
            hidden = jnp.dot(
                inner, up_ref[block, :, c : c + chunk], preferred_element_type=jnp.float32
            )
            parts.append(jax.nn.gelu(hidden, approximate=True).astype(jnp.bfloat16))
        for n, hidden in enumerate(parts):
            downs[block, n].wait()
            state = state + jnp.dot(
                hidden,
                down_ref[block, n * chunk : (n + 1) * chunk, :],
                preferred_element_type=jnp.float32,
            )
    out_ref[...] = lax.dot_general(
        order, state.astype(jnp.bfloat16), TN, preferred_element_type=jnp.float32
    ).astype(out_ref.dtype)


def mix_tracks(rows, place, norm_gains, time_kernels, mix_up, mix_down, tracks):
    def kernel(*refs):
        mixer_kernel(tracks, *refs)

    return pl.pallas_call(
        kernel,
        out_shape=jax.ShapeDtypeStruct(rows.shape, rows.dtype),
        in_specs=[VMEM] * 4 + [HBM, HBM],
        out_specs=VMEM,
        scratch_shapes=[
            pltpu.VMEM(mix_up.shape, mix_up.dtype),
            pltpu.VMEM(mix_down.shape, mix_down.dtype),
            pltpu.SemaphoreType.DMA((2, mix_up.shape[0], pl.cdiv(mix_up.shape[2], 512))),
        ],
        compiler_params=pltpu.CompilerParams(vmem_limit_bytes=53 * MIB),
        name="mixer",
    )(rows, place, norm_gains, time_kernels, mix_up, mix_down)


def on_device(
    features,
    query_frame,
    query_pos,
    frame_order,
    conv1_weight,
    conv1_bias,
    conv2_weight,
    proj_weight,
    norm_gains,
    time_kernels,
    mix_up,
    mix_down,
):
    devices = lax.axis_size(AXIS)
    tracks = query_frame.shape[0] // devices
    side = math.isqrt(features.shape[1])
    grid = math.isqrt(proj_weight.shape[0] // conv2_weight.shape[0])

    def make_tables(args):
        maps, *weights = args
        padded = jnp.pad(maps[0], ((side, side), (0, 0)))
        return padded, conv_tables(*weights, side, grid)

    def order_proj(weight):
        parts = weight.reshape(conv2_weight.shape[0], grid, grid, -1)
        return parts.transpose(1, 0, 2, 3).reshape(weight.shape)

    queries = pick_queries(features, query_frame, query_pos)
    work = (features, conv1_weight, conv1_bias, conv2_weight)
    if devices & (devices - 1):
        queries = lax.psum(queries, AXIS)
        padded, tables = make_tables(work)
        proj = order_proj(proj_weight)
    else:
        stages = exchange_stages(devices)
        queries = exchange(queries, stages[0], devices)
        queries, work = lax.optimization_barrier((queries, work))
        made = make_tables(work)
        queries = exchange(queries, stages[1], devices)
        queries, (padded, tables), proj_weight = lax.optimization_barrier(
            (queries, made, proj_weight)
        )
        proj = order_proj(proj_weight)
        for shifts in stages[2:]:
            queries = exchange(queries, shifts, devices)
    rows = frame_rows(queries, padded, tables, proj, side, grid)
    rows = lax.all_to_all(rows, AXIS, split_axis=0, concat_axis=0, tiled=True)
    place = (frame_order[:, None] * tracks + jnp.arange(tracks, dtype=jnp.int32)).reshape(1, -1)
    mixed = mix_tracks(rows, place, norm_gains, time_kernels, mix_up, mix_down, tracks)
    mixed = lax.all_to_all(mixed, AXIS, split_axis=0, concat_axis=0, tiled=True)
    return mixed[None]


def solution(mesh):
    placed = (
        P(("groups", "frames"), None, None),
        P("groups"),
        P("groups"),
        P("groups"),
        P(),
        P(),
        P(),
        P(),
        P(),
        P(),
        P(),
        P(),
    )
    return jax.shard_map(
        on_device,
        mesh=mesh,
        in_specs=placed,
        out_specs=P(("groups", "frames"), None, None),
        check_vma=False,
    )
```

```python
import math

import jax
import jax.numpy as jnp
from jax import lax
from jax.experimental import pallas as pl
from jax.experimental.pallas import tpu as pltpu
from jax.sharding import PartitionSpec as P

AXIS = "frames"
NT = (((1,), (1,)), ((), ()))
TN = (((0,), (0,)), ((), ()))
VMEM = pl.BlockSpec(memory_space=pltpu.VMEM)
HBM = pl.BlockSpec(memory_space=pltpu.HBM)
MIB = 1024 * 1024


def iota(shape, axis):
    return lax.broadcasted_iota(jnp.int32, shape, axis)


def exchange_stages(devices):
    stages = []
    bit = 1
    while bit < devices:
        if bit == 1 or 2 * bit >= devices:
            stages.append((bit,))
        else:
            stages.append((bit, 2 * bit, 3 * bit))
        bit *= len(stages[-1]) + 1
    return stages


def exchange(values, shifts, devices):
    arrived = [
        lax.ppermute(values, AXIS, [(i, i ^ shift) for i in range(devices)]) for shift in shifts
    ]
    for part in arrived:
        values = values + part
    return values


def pick_kernel(pieces, wanted_ref, feat_hbm, out_ref, feat, sems):
    points, channels = feat.shape
    count = wanted_ref.shape[1]
    piece = points // pieces
    copies = [
        pltpu.make_async_copy(
            feat_hbm.at[0, pl.ds(n * piece, piece)], feat.at[pl.ds(n * piece, piece)], sems.at[n]
        )
        for n in range(pieces)
    ]
    for copy in copies:
        copy.start()
    wanted = jnp.broadcast_to(wanted_ref[...], (count, count)).T
    total = jnp.zeros((count, channels), jnp.float32)
    for n in range(pieces):
        parts = []
        for at in range(n * piece, (n + 1) * piece, count):
            parts.append((wanted == iota((count, count), 1) + at).astype(jnp.bfloat16))
        hot = jnp.concatenate(parts, axis=1)
        copies[n].wait()
        total = total + jnp.dot(
            hot, feat[n * piece : (n + 1) * piece], preferred_element_type=jnp.float32
        )
    out_ref[...] = total.astype(out_ref.dtype)


def pick_queries(features, query_frame, query_pos):
    points, channels = features.shape[1:]
    count = query_frame.shape[0]
    wanted = jnp.where(query_frame == lax.axis_index(AXIS), query_pos, -1)
    pieces = 4

    def kernel(*refs):
        pick_kernel(pieces, *refs)

    return pl.pallas_call(
        kernel,
        out_shape=jax.ShapeDtypeStruct((count, channels), features.dtype),
        in_specs=[VMEM, HBM],
        out_specs=VMEM,
        scratch_shapes=[
            pltpu.VMEM((points, channels), features.dtype),
            pltpu.SemaphoreType.DMA((pieces,)),
        ],
        compiler_params=pltpu.CompilerParams(vmem_limit_bytes=53 * MIB),
        name="pick_queries",
    )(wanted.reshape(1, -1), features)


def tables_kernel(
    side, grid, taps_ref, bias_ref, small_ref, first_ref, lane_bias_ref, second_ref
):
    ch1, ch2 = taps_ref.shape[0], small_ref.shape[1]
    width = side // 2 // grid
    lanes = grid * ch1 * 4
    rows = 4 * side
    hot = (iota((lanes, ch1), 1) == iota((lanes, ch1), 0) // 4 % ch1).astype(jnp.float32)
    lane_bias_ref[...] = jnp.dot(
        hot * bias_ref[...],
        jnp.ones((ch1, lane_bias_ref.shape[1]), jnp.float32),
        precision=lax.Precision.HIGHEST,
        preferred_element_type=jnp.float32,
    )
    hot = hot.astype(jnp.bfloat16)
    taps = [
        jnp.dot(
            hot,
            jnp.broadcast_to(taps_ref[:, n : n + 1], (ch1, rows)).astype(jnp.bfloat16),
            preferred_element_type=jnp.float32,
        )
        for n in range(9)
    ]
    row = iota((lanes, 1), 0)
    at = row // 2 % 2 * rows + 2 * width * (row // (4 * ch1)) + row % 2 - 1
    spot = iota((1, rows), 1)
    diff = spot // side * rows + spot % side - at
    for s in range(width):
        first = jnp.zeros((lanes, rows), jnp.float32)
        for dy in range(3):
            for dx in range(3):
                first = jnp.where(diff == dy * rows + dx + 2 * s, taps[3 * dy + dx], first)
        first_ref[s * lanes : (s + 1) * lanes] = first.astype(jnp.bfloat16)

    outs, ins = second_ref.shape
    group = outs // ch2
    hot = (iota((outs, ch2), 1) == iota((outs, ch2), 0) // group).astype(jnp.bfloat16)
    small = jnp.concatenate([small_ref[...]] * group, axis=0)
    wide = lax.dot_general(hot, small, NT, preferred_element_type=jnp.float32)
    same = iota((outs, ins), 0) % group == iota((outs, ins), 1) // (4 * ch1)
    second_ref[...] = jnp.where(same, wide, 0.0).astype(jnp.bfloat16)


def conv_tables(conv1_weight, conv1_bias, conv2_weight, side, grid):
    ch1 = conv1_weight.shape[0]
    ch2 = conv2_weight.shape[0]
    lanes = grid * ch1 * 4
    group = grid // column_groups(grid, ch1)

    def kernel(*refs):
        tables_kernel(side, grid, *refs)

    return pl.pallas_call(
        kernel,
        out_shape=[
            jax.ShapeDtypeStruct((side // 2 // grid * lanes, 4 * side), jnp.bfloat16),
            jax.ShapeDtypeStruct((lanes, 128), jnp.float32),
            jax.ShapeDtypeStruct((group * ch2, group * ch1 * 4), jnp.bfloat16),
        ],
        in_specs=[VMEM] * 3,
        out_specs=[VMEM] * 3,
        compiler_params=pltpu.CompilerParams(vmem_limit_bytes=24 * MIB),
        name="conv_tables",
    )(conv1_weight, conv1_bias.reshape(1, ch1), conv2_weight.transpose(1, 2, 3, 0).reshape(ch1 * 4, ch2))


def column_groups(grid, ch1):
    return max(1, grid * ch1 * 4 // 256)


def proj_kernel(groups, size, proj_ref, out_ref):
    grid_columns = size
    total, columns = proj_ref.shape
    block = total // grid_columns
    group = grid_columns // groups
    to = iota((block, block), 0)
    per = block // groups
    source = to % per // group * grid_columns + to // per * group + to % group
    move = (iota((block, block), 1) == source).astype(jnp.bfloat16)
    for i in range(total // block):
        at = pl.ds(i * block, block)
        out_ref[at] = jnp.dot(
            move, proj_ref[at], preferred_element_type=jnp.float32
        ).astype(out_ref.dtype)


def order_proj(weight, ch1, ch2, grid):
    parts = weight.reshape(ch2, grid, grid, -1).transpose(1, 0, 2, 3).reshape(weight.shape)

    def kernel(*refs):
        proj_kernel(column_groups(grid, ch1), grid, *refs)

    return pl.pallas_call(
        kernel,
        out_shape=jax.ShapeDtypeStruct(weight.shape, weight.dtype),
        in_specs=[VMEM],
        out_specs=VMEM,
        compiler_params=pltpu.CompilerParams(vmem_limit_bytes=16 * MIB),
        name="order_proj",
    )(parts)


def rows_kernel(
    side, grid, query_ref, feat_ref, first_ref, bias_ref, second_ref, proj_ref, out_ref,
    corr, hold,
):
    half = side // 2
    width = half // grid
    count, channels = query_ref.shape
    points = feat_ref.shape[1]
    scale = 1.0 / math.sqrt(channels)
    step = 2 * side
    edge = jnp.zeros((side, count), corr.dtype)
    corr[pl.ds(0, side)] = edge
    corr[pl.ds(side + points, side)] = edge
    query = query_ref[...]
    piece = min(512, points)
    for at in range(0, points, piece):
        part = lax.dot_general(
            feat_ref[0, at : at + piece], query, NT, preferred_element_type=jnp.float32
        )
        corr[side + at : side + at + piece] = (part * scale).astype(corr.dtype)
    bias = bias_ref[...]
    bias = jnp.concatenate([bias] * (2 * count // bias.shape[1]), axis=1)
    second = second_ref[...]
    lanes = bias.shape[0]
    outs, ins = second.shape
    groups = lanes // ins
    slots = hold.shape[0]
    sums = {}

    def strided(step_number, i):
        for g in range(groups):
            two = jnp.dot(
                second,
                hold[step_number % slots, g * ins : (g + 1) * ins],
                preferred_element_type=jnp.float32,
            )
            two = jnp.maximum(two, 0.0)
            two = two[:, :count] + two[:, count:]
            sums[i, g] = sums[i, g] + two if (i, g) in sums else two

    waiting = []
    for y in range(0, half, 2):
        window = jnp.concatenate([corr[n * step : (n + 2) * step] for n in (y, y + 1)], axis=1)
        for s in range(width):
            one = jnp.dot(
                first_ref[s * lanes : (s + 1) * lanes],
                window,
                preferred_element_type=jnp.float32,
            )
            number = y // 2 * width + s
            hold[number % slots] = jnp.maximum(one + bias, 0.0).astype(jnp.bfloat16)
            waiting.append((number, y // width))
            if len(waiting) > slots // 2:
                strided(*waiting.pop(0))
    for late in waiting:
        strided(*late)
    total = jnp.zeros(out_ref.shape, jnp.float32)
    block = groups * outs
    for i in range(grid):
        pooled = jnp.concatenate([sums[i, g] for g in range(groups)], axis=0)
        pooled = (pooled * (1.0 / (width * width))).astype(jnp.bfloat16)
        total = total + lax.dot_general(
            pooled,
            proj_ref[i * block : (i + 1) * block],
            TN,
            preferred_element_type=jnp.float32,
        )
    out_ref[...] = total.astype(out_ref.dtype)


def frame_rows(queries, features, tables, proj, side, grid):
    count = queries.shape[0]

    def kernel(*refs):
        rows_kernel(side, grid, *refs)

    return pl.pallas_call(
        kernel,
        out_shape=jax.ShapeDtypeStruct((count, proj.shape[1]), jnp.bfloat16),
        in_specs=[VMEM] * 6,
        out_specs=VMEM,
        scratch_shapes=[
            pltpu.VMEM((features.shape[1] + 2 * side, count), jnp.bfloat16),
            pltpu.VMEM((8, tables[1].shape[0], 2 * count), jnp.bfloat16),
        ],
        compiler_params=pltpu.CompilerParams(vmem_limit_bytes=32 * MIB),
        name="frame_rows",
    )(queries, features, *tables, proj)


def layer_norm(values):
    center = values - jnp.mean(values, axis=-1, keepdims=True)
    spread = jnp.mean(center * center, axis=-1, keepdims=True)
    return center * lax.rsqrt(spread + 1e-05)


def mixer_kernel(
    tracks, rows_ref, place_ref, gain_ref, time_ref, up_hbm, down_hbm, out_ref, up_ref, down_ref, sems
):
    blocks, width, hidden_size = up_hbm.shape
    chunk = min(1024, hidden_size)
    starts = range(0, hidden_size, chunk)
    ups, downs = {}, {}
    for block in range(blocks):
        for n, c in enumerate(starts):
            at = (block, slice(None), pl.ds(c, chunk))
            ups[block, n] = pltpu.make_async_copy(
                up_hbm.at[at], up_ref.at[at], sems.at[0, block, n]
            )
            ups[block, n].start()
        for n, c in enumerate(starts):
            at = (block, pl.ds(c, chunk))
            downs[block, n] = pltpu.make_async_copy(
                down_hbm.at[at], down_ref.at[at], sems.at[1, block, n]
            )
            downs[block, n].start()
    length = rows_ref.shape[0]
    frames = place_ref.shape[1]
    spread = (iota((frames, length), 0) == iota((frames, length), 1) // tracks).astype(jnp.float32)
    time = jnp.dot(
        jnp.broadcast_to(place_ref[...].astype(jnp.float32), (8, frames)),
        spread,
        preferred_element_type=jnp.float32,
    )[0:1]
    place = time.astype(jnp.int32) * tracks + iota((1, length), 1) % tracks
    order = (iota((length, length), 0) == place).astype(jnp.bfloat16)
    state = jnp.dot(order, rows_ref[...], preferred_element_type=jnp.float32)
    edge = jnp.zeros((tracks, width), jnp.float32)
    for block in range(blocks):
        normed = layer_norm(state) * gain_ref[block, 0:1]
        before = jnp.concatenate([edge, normed[:-tracks]], axis=0)
        after = jnp.concatenate([normed[tracks:], edge], axis=0)
        state = (
            state
            + time_ref[0, block : block + 1] * before
            + time_ref[1, block : block + 1] * normed
            + time_ref[2, block : block + 1] * after
        )
        inner = (layer_norm(state) * gain_ref[block, 1:2]).astype(jnp.bfloat16)
        parts = []
        for n, c in enumerate(starts):
            ups[block, n].wait()
            hidden = jnp.dot(
                inner, up_ref[block, :, c : c + chunk], preferred_element_type=jnp.float32
            )
            parts.append(jax.nn.gelu(hidden, approximate=True).astype(jnp.bfloat16))
        for n, hidden in enumerate(parts):
            downs[block, n].wait()
            state = state + jnp.dot(
                hidden,
                down_ref[block, n * chunk : (n + 1) * chunk, :],
                preferred_element_type=jnp.float32,
            )
    out_ref[...] = lax.dot_general(
        order, state.astype(jnp.bfloat16), TN, preferred_element_type=jnp.float32
    ).astype(out_ref.dtype)


def mix_tracks(rows, place, norm_gains, time_kernels, mix_up, mix_down, tracks):
    def kernel(*refs):
        mixer_kernel(tracks, *refs)

    return pl.pallas_call(
        kernel,
        out_shape=jax.ShapeDtypeStruct(rows.shape, rows.dtype),
        in_specs=[VMEM] * 4 + [HBM, HBM],
        out_specs=VMEM,
        scratch_shapes=[
            pltpu.VMEM(mix_up.shape, mix_up.dtype),
            pltpu.VMEM(mix_down.shape, mix_down.dtype),
            pltpu.SemaphoreType.DMA((2, mix_up.shape[0], pl.cdiv(mix_up.shape[2], 1024))),
        ],
        compiler_params=pltpu.CompilerParams(vmem_limit_bytes=53 * MIB),
        name="mixer",
    )(rows, place, norm_gains, time_kernels, mix_up, mix_down)


def on_device(
    features,
    query_frame,
    query_pos,
    frame_order,
    conv1_weight,
    conv1_bias,
    conv2_weight,
    proj_weight,
    norm_gains,
    time_kernels,
    mix_up,
    mix_down,
):
    devices = lax.axis_size(AXIS)
    tracks = query_frame.shape[0] // devices
    side = math.isqrt(features.shape[1])
    grid = math.isqrt(proj_weight.shape[0] // conv2_weight.shape[0])

    queries = pick_queries(features, query_frame, query_pos)
    ch1, ch2 = conv1_weight.shape[0], conv2_weight.shape[0]
    convs = (conv1_weight, conv1_bias, conv2_weight)
    if devices & (devices - 1):
        queries = lax.psum(queries, AXIS)
        tables = conv_tables(*convs, side, grid)
        proj = order_proj(proj_weight, ch1, ch2, grid)
    else:
        stages = exchange_stages(devices)
        queries = exchange(queries, stages[0], devices)
        queries, convs = lax.optimization_barrier((queries, convs))
        tables = conv_tables(*convs, side, grid)
        queries = exchange(queries, stages[1], devices)
        queries, tables, proj_weight = lax.optimization_barrier((queries, tables, proj_weight))
        proj = order_proj(proj_weight, ch1, ch2, grid)
        for shifts in stages[2:]:
            queries = exchange(queries, shifts, devices)
    rows = frame_rows(queries, features, tables, proj, side, grid)
    rows = lax.all_to_all(rows, AXIS, split_axis=0, concat_axis=0, tiled=True)
    place = frame_order.reshape(1, -1)
    mixed = mix_tracks(rows, place, norm_gains, time_kernels.transpose(1, 0, 2), mix_up, mix_down, tracks)
    mixed = lax.all_to_all(mixed, AXIS, split_axis=0, concat_axis=0, tiled=True)
    return mixed[None]


def solution(mesh):
    placed = (
        P(("groups", "frames"), None, None),
        P("groups"),
        P("groups"),
        P("groups"),
        P(),
        P(),
        P(),
        P(),
        P(),
        P(),
        P(),
        P(),
    )
    return jax.shard_map(
        on_device,
        mesh=mesh,
        in_specs=placed,
        out_specs=P(("groups", "frames"), None, None),
        check_vma=False,
    )
```

```python
import math

import jax
import jax.numpy as jnp
from jax import lax
from jax.experimental import pallas as pl
from jax.experimental.pallas import tpu as pltpu
from jax.sharding import PartitionSpec as P

AXIS = "frames"
NT = (((1,), (1,)), ((), ()))
TN = (((0,), (0,)), ((), ()))
VMEM = pl.BlockSpec(memory_space=pltpu.VMEM)
HBM = pl.BlockSpec(memory_space=pltpu.HBM)
MIB = 1024 * 1024


def iota(shape, axis):
    return lax.broadcasted_iota(jnp.int32, shape, axis)


def exchange_stages(devices):
    stages = []
    bit = 2
    while bit < devices:
        stages.append((bit,) if 2 * bit >= devices else (bit, 2 * bit, 3 * bit))
        bit *= len(stages[-1]) + 1
    return stages


def exchange(values, shifts, devices):
    arrived = [
        lax.ppermute(values, AXIS, [(i, i ^ shift) for i in range(devices)]) for shift in shifts
    ]
    for part in arrived:
        values = values + part
    return values


def pick_kernel(wanted_ref, feat_ref, mine_ref, other_ref):
    points = feat_ref.shape[1]
    count = wanted_ref.shape[1]
    wanted = jnp.broadcast_to(wanted_ref[...], (count, count)).T
    spots = iota((count, count), 1)
    hot = jnp.concatenate(
        [(wanted == spots + at).astype(jnp.bfloat16) for at in range(0, points, count)], axis=1
    )
    total = jnp.dot(hot, feat_ref[0], preferred_element_type=jnp.float32).astype(mine_ref.dtype)
    low, high = total[: count // 2], total[count // 2 :]
    even = lax.axis_index(AXIS) % 2 == 0
    mine_ref[...] = jnp.where(even, low, high)
    other_ref[...] = jnp.where(even, high, low)


def pick_queries(features, query_frame, query_pos):
    count = query_frame.shape[0]
    wanted = jnp.where(query_frame == lax.axis_index(AXIS), query_pos, -1)
    return pl.pallas_call(
        pick_kernel,
        out_shape=[jax.ShapeDtypeStruct((count // 2, features.shape[2]), features.dtype)] * 2,
        in_specs=[VMEM, VMEM],
        out_specs=[VMEM, VMEM],
        compiler_params=pltpu.CompilerParams(vmem_limit_bytes=16 * MIB),
        name="pick_queries",
    )(wanted.reshape(1, -1), features)


def tables_kernel(
    side, grid, taps_ref, bias_ref, small_ref, first_ref, lane_bias_ref, second_ref
):
    ch1, ch2 = taps_ref.shape[0], small_ref.shape[1]
    width = side // 2 // grid
    lanes = grid * ch1 * 4
    rows = 4 * side
    hot = (iota((lanes, ch1), 1) == iota((lanes, ch1), 0) // 4 % ch1).astype(jnp.float32)
    lane_bias_ref[...] = jnp.dot(
        hot * bias_ref[...],
        jnp.ones((ch1, lane_bias_ref.shape[1]), jnp.float32),
        precision=lax.Precision.HIGHEST,
        preferred_element_type=jnp.float32,
    )
    hot = hot.astype(jnp.bfloat16)
    taps = [
        jnp.dot(
            hot,
            jnp.broadcast_to(taps_ref[:, n : n + 1], (ch1, rows)).astype(jnp.bfloat16),
            preferred_element_type=jnp.float32,
        )
        for n in range(9)
    ]
    row = iota((lanes, 1), 0)
    at = row // 2 % 2 * rows + 2 * width * (row // (4 * ch1)) + row % 2 - 1
    spot = iota((1, rows), 1)
    diff = spot // side * rows + spot % side - at
    for s in range(width):
        first = jnp.zeros((lanes, rows), jnp.float32)
        for dy in range(3):
            for dx in range(3):
                first = jnp.where(diff == dy * rows + dx + 2 * s, taps[3 * dy + dx], first)
        first_ref[s * lanes : (s + 1) * lanes] = first.astype(jnp.bfloat16)

    outs, ins = second_ref.shape
    group = outs // ch2
    hot = (iota((outs, ch2), 1) == iota((outs, ch2), 0) // group).astype(jnp.bfloat16)
    small = jnp.concatenate([small_ref[...]] * group, axis=0)
    wide = lax.dot_general(hot, small, NT, preferred_element_type=jnp.float32)
    same = iota((outs, ins), 0) % group == iota((outs, ins), 1) // (4 * ch1)
    second_ref[...] = jnp.where(same, wide, 0.0).astype(jnp.bfloat16)


def conv_tables(conv1_weight, conv1_bias, conv2_weight, side, grid):
    ch1 = conv1_weight.shape[0]
    ch2 = conv2_weight.shape[0]
    lanes = grid * ch1 * 4
    group = grid // column_groups(grid, ch1)

    def kernel(*refs):
        tables_kernel(side, grid, *refs)

    return pl.pallas_call(
        kernel,
        out_shape=[
            jax.ShapeDtypeStruct((side // 2 // grid * lanes, 4 * side), jnp.bfloat16),
            jax.ShapeDtypeStruct((lanes, 128), jnp.float32),
            jax.ShapeDtypeStruct((group * ch2, group * ch1 * 4), jnp.bfloat16),
        ],
        in_specs=[VMEM] * 3,
        out_specs=[VMEM] * 3,
        compiler_params=pltpu.CompilerParams(vmem_limit_bytes=24 * MIB),
        name="conv_tables",
    )(conv1_weight, conv1_bias.reshape(1, ch1), conv2_weight.transpose(1, 2, 3, 0).reshape(ch1 * 4, ch2))


def column_groups(grid, ch1):
    return max(1, grid * ch1 * 4 // 256)


def proj_kernel(groups, size, proj_ref, out_ref):
    grid_columns = size
    total, columns = proj_ref.shape
    block = total // grid_columns
    group = grid_columns // groups
    to = iota((block, block), 0)
    per = block // groups
    source = to % per // group * grid_columns + to // per * group + to % group
    move = (iota((block, block), 1) == source).astype(jnp.bfloat16)
    for i in range(total // block):
        at = pl.ds(i * block, block)
        out_ref[at] = jnp.dot(
            move, proj_ref[at], preferred_element_type=jnp.float32
        ).astype(out_ref.dtype)


def order_proj(weight, ch1, ch2, grid):
    parts = weight.reshape(ch2, grid, grid, -1).transpose(1, 0, 2, 3).reshape(weight.shape)

    def kernel(*refs):
        proj_kernel(column_groups(grid, ch1), grid, *refs)

    return pl.pallas_call(
        kernel,
        out_shape=jax.ShapeDtypeStruct(weight.shape, weight.dtype),
        in_specs=[VMEM],
        out_specs=VMEM,
        compiler_params=pltpu.CompilerParams(vmem_limit_bytes=16 * MIB),
        name="order_proj",
    )(parts)


def rows_kernel(
    side, grid, mine_ref, other_ref, feat_ref, first_ref, bias_ref, second_ref, proj_ref, out_ref,
    corr, hold,
):
    half = side // 2
    width = half // grid
    mine, other = mine_ref[...], other_ref[...]
    even = lax.axis_index(AXIS) % 2 == 0
    query = jnp.concatenate([jnp.where(even, mine, other), jnp.where(even, other, mine)], axis=0)
    count, channels = query.shape
    points = feat_ref.shape[1]
    scale = 1.0 / math.sqrt(channels)
    step = 2 * side
    edge = jnp.zeros((side, count), corr.dtype)
    corr[pl.ds(0, side)] = edge
    corr[pl.ds(side + points, side)] = edge
    piece = min(512, points)
    for at in range(0, points, piece):
        part = lax.dot_general(
            feat_ref[0, at : at + piece], query, NT, preferred_element_type=jnp.float32
        )
        corr[side + at : side + at + piece] = (part * scale).astype(corr.dtype)
    bias = bias_ref[...]
    bias = jnp.concatenate([bias] * (2 * count // bias.shape[1]), axis=1)
    second = second_ref[...]
    lanes = bias.shape[0]
    outs, ins = second.shape
    groups = lanes // ins
    slots = hold.shape[0]
    sums = {}

    def strided(step_number, i):
        for g in range(groups):
            two = jnp.dot(
                second,
                hold[step_number % slots, g * ins : (g + 1) * ins],
                preferred_element_type=jnp.float32,
            )
            two = jnp.maximum(two, 0.0)
            two = two[:, :count] + two[:, count:]
            sums[i, g] = sums[i, g] + two if (i, g) in sums else two

    waiting = []
    for y in range(0, half, 2):
        window = jnp.concatenate([corr[n * step : (n + 2) * step] for n in (y, y + 1)], axis=1)
        for s in range(width):
            one = jnp.dot(
                first_ref[s * lanes : (s + 1) * lanes],
                window,
                preferred_element_type=jnp.float32,
            )
            number = y // 2 * width + s
            hold[number % slots] = jnp.maximum(one + bias, 0.0).astype(jnp.bfloat16)
            waiting.append((number, y // width))
            if len(waiting) > slots // 2:
                strided(*waiting.pop(0))
    for late in waiting:
        strided(*late)
    total = jnp.zeros(out_ref.shape, jnp.float32)
    block = groups * outs
    for i in range(grid):
        pooled = jnp.concatenate([sums[i, g] for g in range(groups)], axis=0)
        pooled = (pooled * (1.0 / (width * width))).astype(jnp.bfloat16)
        total = total + lax.dot_general(
            pooled,
            proj_ref[i * block : (i + 1) * block],
            TN,
            preferred_element_type=jnp.float32,
        )
    out_ref[...] = total.astype(out_ref.dtype)


def frame_rows(mine, other, features, tables, proj, side, grid):
    count = 2 * mine.shape[0]

    def kernel(*refs):
        rows_kernel(side, grid, *refs)

    return pl.pallas_call(
        kernel,
        out_shape=jax.ShapeDtypeStruct((count, proj.shape[1]), jnp.bfloat16),
        in_specs=[VMEM] * 7,
        out_specs=VMEM,
        scratch_shapes=[
            pltpu.VMEM((features.shape[1] + 2 * side, count), jnp.bfloat16),
            pltpu.VMEM((8, tables[1].shape[0], 2 * count), jnp.bfloat16),
        ],
        compiler_params=pltpu.CompilerParams(vmem_limit_bytes=32 * MIB),
        name="frame_rows",
    )(mine, other, features, *tables, proj)


def layer_norm(values):
    center = values - jnp.mean(values, axis=-1, keepdims=True)
    spread = jnp.mean(center * center, axis=-1, keepdims=True)
    return center * lax.rsqrt(spread + 1e-05)


def mixer_kernel(
    tracks, rows_ref, place_ref, gain_ref, time_ref, up_hbm, down_hbm, out_ref, up_ref, down_ref, sems
):
    blocks, width, hidden_size = up_hbm.shape
    chunk = min(1024, hidden_size)
    starts = range(0, hidden_size, chunk)
    ups, downs = {}, {}
    for block in range(blocks):
        for n, c in enumerate(starts):
            at = (block, slice(None), pl.ds(c, chunk))
            ups[block, n] = pltpu.make_async_copy(
                up_hbm.at[at], up_ref.at[at], sems.at[0, block, n]
            )
            ups[block, n].start()
        for n, c in enumerate(starts):
            at = (block, pl.ds(c, chunk))
            downs[block, n] = pltpu.make_async_copy(
                down_hbm.at[at], down_ref.at[at], sems.at[1, block, n]
            )
            downs[block, n].start()
    length = rows_ref.shape[0]
    frames = place_ref.shape[1]
    spread = (iota((frames, length), 0) == iota((frames, length), 1) // tracks).astype(jnp.float32)
    time = jnp.dot(
        jnp.broadcast_to(place_ref[...].astype(jnp.float32), (8, frames)),
        spread,
        preferred_element_type=jnp.float32,
    )[0:1]
    place = time.astype(jnp.int32) * tracks + iota((1, length), 1) % tracks
    order = (iota((length, length), 0) == place).astype(jnp.bfloat16)
    state = jnp.dot(order, rows_ref[...], preferred_element_type=jnp.float32)
    edge = jnp.zeros((tracks, width), jnp.float32)
    for block in range(blocks):
        normed = layer_norm(state) * gain_ref[block, 0:1]
        before = jnp.concatenate([edge, normed[:-tracks]], axis=0)
        after = jnp.concatenate([normed[tracks:], edge], axis=0)
        state = (
            state
            + time_ref[0, block : block + 1] * before
            + time_ref[1, block : block + 1] * normed
            + time_ref[2, block : block + 1] * after
        )
        inner = (layer_norm(state) * gain_ref[block, 1:2]).astype(jnp.bfloat16)
        parts = []
        for n, c in enumerate(starts):
            ups[block, n].wait()
            hidden = jnp.dot(
                inner, up_ref[block, :, c : c + chunk], preferred_element_type=jnp.float32
            )
            parts.append(jax.nn.gelu(hidden, approximate=True).astype(jnp.bfloat16))
        for n, hidden in enumerate(parts):
            downs[block, n].wait()
            state = state + jnp.dot(
                hidden,
                down_ref[block, n * chunk : (n + 1) * chunk, :],
                preferred_element_type=jnp.float32,
            )
    out_ref[...] = lax.dot_general(
        order, state.astype(jnp.bfloat16), TN, preferred_element_type=jnp.float32
    ).astype(out_ref.dtype)


def mix_tracks(rows, place, norm_gains, time_kernels, mix_up, mix_down, tracks):
    def kernel(*refs):
        mixer_kernel(tracks, *refs)

    return pl.pallas_call(
        kernel,
        out_shape=jax.ShapeDtypeStruct(rows.shape, rows.dtype),
        in_specs=[VMEM] * 4 + [HBM, HBM],
        out_specs=VMEM,
        scratch_shapes=[
            pltpu.VMEM(mix_up.shape, mix_up.dtype),
            pltpu.VMEM(mix_down.shape, mix_down.dtype),
            pltpu.SemaphoreType.DMA((2, mix_up.shape[0], pl.cdiv(mix_up.shape[2], 1024))),
        ],
        compiler_params=pltpu.CompilerParams(vmem_limit_bytes=53 * MIB),
        name="mixer",
    )(rows, place, norm_gains, time_kernels, mix_up, mix_down)


def on_device(
    features,
    query_frame,
    query_pos,
    frame_order,
    conv1_weight,
    conv1_bias,
    conv2_weight,
    proj_weight,
    norm_gains,
    time_kernels,
    mix_up,
    mix_down,
):
    devices = lax.axis_size(AXIS)
    tracks = query_frame.shape[0] // devices
    side = math.isqrt(features.shape[1])
    grid = math.isqrt(proj_weight.shape[0] // conv2_weight.shape[0])

    mine, other = pick_queries(features, query_frame, query_pos)
    ch1, ch2 = conv1_weight.shape[0], conv2_weight.shape[0]
    convs = (conv1_weight, conv1_bias, conv2_weight)
    if devices & (devices - 1):
        even = lax.axis_index(AXIS) % 2 == 0
        half = mine.shape[0]
        both = jnp.concatenate([jnp.where(even, mine, other), jnp.where(even, other, mine)], axis=0)
        both = lax.psum(both, AXIS)
        mine = jnp.where(even, both[:half], both[half:])
        other = jnp.where(even, both[half:], both[:half])
        tables = conv_tables(*convs, side, grid)
        proj = order_proj(proj_weight, ch1, ch2, grid)
    else:
        swap = [(i, i ^ 1) for i in range(devices)]
        mine = mine + lax.ppermute(other, AXIS, swap)
        mine, convs = lax.optimization_barrier((mine, convs))
        tables = conv_tables(*convs, side, grid)
        stages = exchange_stages(devices)
        mine = exchange(mine, stages[0], devices)
        mine, tables, proj_weight = lax.optimization_barrier((mine, tables, proj_weight))
        proj = order_proj(proj_weight, ch1, ch2, grid)
        for shifts in stages[1:]:
            mine = exchange(mine, shifts, devices)
        mine, proj = lax.optimization_barrier((mine, proj))
        other = lax.ppermute(mine, AXIS, swap)
    rows = frame_rows(mine, other, features, tables, proj, side, grid)
    rows = lax.all_to_all(rows, AXIS, split_axis=0, concat_axis=0, tiled=True)
    place = frame_order.reshape(1, -1)
    mixed = mix_tracks(rows, place, norm_gains, time_kernels.transpose(1, 0, 2), mix_up, mix_down, tracks)
    mixed = lax.all_to_all(mixed, AXIS, split_axis=0, concat_axis=0, tiled=True)
    return mixed[None]


def solution(mesh):
    placed = (
        P(("groups", "frames"), None, None),
        P("groups"),
        P("groups"),
        P("groups"),
        P(),
        P(),
        P(),
        P(),
        P(),
        P(),
        P(),
        P(),
    )
    return jax.shard_map(
        on_device,
        mesh=mesh,
        in_specs=placed,
        out_specs=P(("groups", "frames"), None, None),
        check_vma=False,
    )
```

```python
import math

import jax
import jax.numpy as jnp
from jax import lax
from jax.experimental import pallas as pl
from jax.experimental.pallas import tpu as pltpu
from jax.sharding import PartitionSpec as P

AXIS = "frames"
NT = (((1,), (1,)), ((), ()))
TN = (((0,), (0,)), ((), ()))
VMEM = pl.BlockSpec(memory_space=pltpu.VMEM)
HBM = pl.BlockSpec(memory_space=pltpu.HBM)
MIB = 1024 * 1024


def iota(shape, axis):
    return lax.broadcasted_iota(jnp.int32, shape, axis)


def exchange_stages(devices):
    stages = []
    bit = 2
    while bit < devices:
        if 2 * bit >= devices:
            stages.append((bit,))
        elif stages:
            stages.append((2 * bit, bit, 3 * bit))
        else:
            stages.append((bit, 2 * bit, 3 * bit))
        bit *= len(stages[-1]) + 1
    return stages


def exchange(values, shifts, devices):
    arrived = [
        lax.ppermute(values, AXIS, [(i, i ^ shift) for i in range(devices)]) for shift in shifts
    ]
    for part in arrived:
        values = values + part
    return values


def pick_kernel(wanted_ref, feat_ref, mine_ref, other_ref):
    points = feat_ref.shape[1]
    count = wanted_ref.shape[1]
    wanted = jnp.broadcast_to(wanted_ref[...], (count, count)).T
    spots = iota((count, count), 1)
    hot = jnp.concatenate(
        [(wanted == spots + at).astype(jnp.bfloat16) for at in range(0, points, count)], axis=1
    )
    total = jnp.dot(hot, feat_ref[0], preferred_element_type=jnp.float32).astype(mine_ref.dtype)
    low, high = total[: count // 2], total[count // 2 :]
    even = lax.axis_index(AXIS) % 2 == 0
    mine_ref[...] = jnp.where(even, low, high)
    other_ref[...] = jnp.where(even, high, low)


def pick_queries(features, query_frame, query_pos):
    count = query_frame.shape[0]
    wanted = jnp.where(query_frame == lax.axis_index(AXIS), query_pos, -1)
    return pl.pallas_call(
        pick_kernel,
        out_shape=[jax.ShapeDtypeStruct((count // 2, features.shape[2]), features.dtype)] * 2,
        in_specs=[VMEM, VMEM],
        out_specs=[VMEM, VMEM],
        compiler_params=pltpu.CompilerParams(vmem_limit_bytes=16 * MIB),
        name="pick_queries",
    )(wanted.reshape(1, -1), features)


def tables_kernel(
    side, grid, taps_ref, bias_ref, small_ref, first_ref, lane_bias_ref, second_ref
):
    ch1, ch2 = taps_ref.shape[0], small_ref.shape[1]
    width = side // 2 // grid
    lanes = grid * ch1 * 4
    rows = 4 * side
    hot = (iota((lanes, ch1), 1) == iota((lanes, ch1), 0) // 4 % ch1).astype(jnp.float32)
    lane_bias_ref[...] = jnp.dot(
        hot * bias_ref[...],
        jnp.ones((ch1, lane_bias_ref.shape[1]), jnp.float32),
        precision=lax.Precision.HIGHEST,
        preferred_element_type=jnp.float32,
    )
    hot = hot.astype(jnp.bfloat16)
    taps = [
        jnp.dot(
            hot,
            jnp.broadcast_to(taps_ref[:, n : n + 1], (ch1, rows)).astype(jnp.bfloat16),
            preferred_element_type=jnp.float32,
        )
        for n in range(9)
    ]
    row = iota((lanes, 1), 0)
    at = row // 2 % 2 * rows + 2 * width * (row // (4 * ch1)) + row % 2 - 1
    spot = iota((1, rows), 1)
    diff = spot // side * rows + spot % side - at
    for s in range(width):
        first = jnp.zeros((lanes, rows), jnp.float32)
        for dy in range(3):
            for dx in range(3):
                first = jnp.where(diff == dy * rows + dx + 2 * s, taps[3 * dy + dx], first)
        first_ref[s * lanes : (s + 1) * lanes] = first.astype(jnp.bfloat16)

    outs, ins = second_ref.shape
    group = outs // ch2
    hot = (iota((outs, ch2), 1) == iota((outs, ch2), 0) // group).astype(jnp.bfloat16)
    small = jnp.concatenate([small_ref[...]] * group, axis=0)
    wide = lax.dot_general(hot, small, NT, preferred_element_type=jnp.float32)
    same = iota((outs, ins), 0) % group == iota((outs, ins), 1) // (4 * ch1)
    second_ref[...] = jnp.where(same, wide, 0.0).astype(jnp.bfloat16)


def conv_tables(conv1_weight, conv1_bias, conv2_weight, side, grid):
    ch1 = conv1_weight.shape[0]
    ch2 = conv2_weight.shape[0]
    lanes = grid * ch1 * 4
    group = grid // column_groups(grid, ch1)

    def kernel(*refs):
        tables_kernel(side, grid, *refs)

    return pl.pallas_call(
        kernel,
        out_shape=[
            jax.ShapeDtypeStruct((side // 2 // grid * lanes, 4 * side), jnp.bfloat16),
            jax.ShapeDtypeStruct((lanes, 128), jnp.float32),
            jax.ShapeDtypeStruct((group * ch2, group * ch1 * 4), jnp.bfloat16),
        ],
        in_specs=[VMEM] * 3,
        out_specs=[VMEM] * 3,
        compiler_params=pltpu.CompilerParams(vmem_limit_bytes=24 * MIB),
        name="conv_tables",
    )(conv1_weight, conv1_bias.reshape(1, ch1), conv2_weight.transpose(1, 2, 3, 0).reshape(ch1 * 4, ch2))


def column_groups(grid, ch1):
    return max(1, grid * ch1 * 4 // 256)


def proj_kernel(groups, size, proj_ref, out_ref):
    grid_columns = size
    total, columns = proj_ref.shape
    block = total // grid_columns
    group = grid_columns // groups
    to = iota((block, block), 0)
    per = block // groups
    source = to % per // group * grid_columns + to // per * group + to % group
    move = (iota((block, block), 1) == source).astype(jnp.bfloat16)
    for i in range(total // block):
        at = pl.ds(i * block, block)
        out_ref[at] = jnp.dot(
            move, proj_ref[at], preferred_element_type=jnp.float32
        ).astype(out_ref.dtype)


def order_proj(weight, ch1, ch2, grid):
    parts = weight.reshape(ch2, grid, grid, -1).transpose(1, 0, 2, 3).reshape(weight.shape)

    def kernel(*refs):
        proj_kernel(column_groups(grid, ch1), grid, *refs)

    return pl.pallas_call(
        kernel,
        out_shape=jax.ShapeDtypeStruct(weight.shape, weight.dtype),
        in_specs=[VMEM],
        out_specs=VMEM,
        compiler_params=pltpu.CompilerParams(vmem_limit_bytes=16 * MIB),
        name="order_proj",
    )(parts)


def rows_kernel(
    side, grid, mine_ref, other_ref, feat_ref, first_ref, bias_ref, second_ref, proj_ref, out_ref,
    corr, hold,
):
    half = side // 2
    width = half // grid
    mine, other = mine_ref[...], other_ref[...]
    even = lax.axis_index(AXIS) % 2 == 0
    query = jnp.concatenate([jnp.where(even, mine, other), jnp.where(even, other, mine)], axis=0)
    count, channels = query.shape
    points = feat_ref.shape[1]
    scale = 1.0 / math.sqrt(channels)
    step = 2 * side
    edge = jnp.zeros((side, count), corr.dtype)
    corr[pl.ds(0, side)] = edge
    corr[pl.ds(side + points, side)] = edge
    piece = min(512, points)
    for at in range(0, points, piece):
        part = lax.dot_general(
            feat_ref[0, at : at + piece], query, NT, preferred_element_type=jnp.float32
        )
        corr[side + at : side + at + piece] = (part * scale).astype(corr.dtype)
    bias = bias_ref[...]
    bias = jnp.concatenate([bias] * (2 * count // bias.shape[1]), axis=1)
    second = second_ref[...]
    lanes = bias.shape[0]
    outs, ins = second.shape
    groups = lanes // ins
    slots = hold.shape[0]
    sums = {}

    def strided(step_number, i):
        for g in range(groups):
            two = jnp.dot(
                second,
                hold[step_number % slots, g * ins : (g + 1) * ins],
                preferred_element_type=jnp.float32,
            )
            two = jnp.maximum(two, 0.0)
            two = two[:, :count] + two[:, count:]
            sums[i, g] = sums[i, g] + two if (i, g) in sums else two

    waiting = []
    for y in range(0, half, 2):
        window = jnp.concatenate([corr[n * step : (n + 2) * step] for n in (y, y + 1)], axis=1)
        for s in range(width):
            one = jnp.dot(
                first_ref[s * lanes : (s + 1) * lanes],
                window,
                preferred_element_type=jnp.float32,
            )
            number = y // 2 * width + s
            hold[number % slots] = jnp.maximum(one + bias, 0.0).astype(jnp.bfloat16)
            waiting.append((number, y // width))
            if len(waiting) > slots // 2:
                strided(*waiting.pop(0))
    for late in waiting:
        strided(*late)
    total = jnp.zeros(out_ref.shape, jnp.float32)
    block = groups * outs
    for i in range(grid):
        pooled = jnp.concatenate([sums[i, g] for g in range(groups)], axis=0)
        pooled = (pooled * (1.0 / (width * width))).astype(jnp.bfloat16)
        total = total + lax.dot_general(
            pooled,
            proj_ref[i * block : (i + 1) * block],
            TN,
            preferred_element_type=jnp.float32,
        )
    out_ref[...] = total.astype(out_ref.dtype)


def frame_rows(mine, other, features, tables, proj, side, grid):
    count = 2 * mine.shape[0]

    def kernel(*refs):
        rows_kernel(side, grid, *refs)

    return pl.pallas_call(
        kernel,
        out_shape=jax.ShapeDtypeStruct((count, proj.shape[1]), jnp.bfloat16),
        in_specs=[VMEM] * 7,
        out_specs=VMEM,
        scratch_shapes=[
            pltpu.VMEM((features.shape[1] + 2 * side, count), jnp.bfloat16),
            pltpu.VMEM((8, tables[1].shape[0], 2 * count), jnp.bfloat16),
        ],
        compiler_params=pltpu.CompilerParams(vmem_limit_bytes=32 * MIB),
        name="frame_rows",
    )(mine, other, features, *tables, proj)


def layer_norm(values):
    center = values - jnp.mean(values, axis=-1, keepdims=True)
    spread = jnp.mean(center * center, axis=-1, keepdims=True)
    return center * lax.rsqrt(spread + 1e-05)


def mixer_kernel(
    tracks, rows_ref, place_ref, gain_ref, time_ref, up_hbm, down_hbm, out_ref, up_ref, down_ref, sems
):
    blocks, width, hidden_size = up_hbm.shape
    chunk = min(1024, hidden_size)
    starts = range(0, hidden_size, chunk)
    ups, downs = {}, {}
    for block in range(blocks):
        for n, c in enumerate(starts):
            at = (block, slice(None), pl.ds(c, chunk))
            ups[block, n] = pltpu.make_async_copy(
                up_hbm.at[at], up_ref.at[at], sems.at[0, block, n]
            )
            ups[block, n].start()
        for n, c in enumerate(starts):
            at = (block, pl.ds(c, chunk))
            downs[block, n] = pltpu.make_async_copy(
                down_hbm.at[at], down_ref.at[at], sems.at[1, block, n]
            )
            downs[block, n].start()
    length = rows_ref.shape[0]
    frames = place_ref.shape[1]
    spread = (iota((frames, length), 0) == iota((frames, length), 1) // tracks).astype(jnp.float32)
    time = jnp.dot(
        jnp.broadcast_to(place_ref[...].astype(jnp.float32), (8, frames)),
        spread,
        preferred_element_type=jnp.float32,
    )[0:1]
    place = time.astype(jnp.int32) * tracks + iota((1, length), 1) % tracks
    order = (iota((length, length), 0) == place).astype(jnp.bfloat16)
    state = jnp.dot(order, rows_ref[...], preferred_element_type=jnp.float32)
    edge = jnp.zeros((tracks, width), jnp.float32)
    for block in range(blocks):
        normed = layer_norm(state) * gain_ref[block, 0:1]
        before = jnp.concatenate([edge, normed[:-tracks]], axis=0)
        after = jnp.concatenate([normed[tracks:], edge], axis=0)
        state = (
            state
            + time_ref[0, block : block + 1] * before
            + time_ref[1, block : block + 1] * normed
            + time_ref[2, block : block + 1] * after
        )
        inner = (layer_norm(state) * gain_ref[block, 1:2]).astype(jnp.bfloat16)
        parts = []
        for n, c in enumerate(starts):
            ups[block, n].wait()
            hidden = jnp.dot(
                inner, up_ref[block, :, c : c + chunk], preferred_element_type=jnp.float32
            )
            parts.append(jax.nn.gelu(hidden, approximate=True).astype(jnp.bfloat16))
        for n, hidden in enumerate(parts):
            downs[block, n].wait()
            state = state + jnp.dot(
                hidden,
                down_ref[block, n * chunk : (n + 1) * chunk, :],
                preferred_element_type=jnp.float32,
            )
    out_ref[...] = lax.dot_general(
        order, state.astype(jnp.bfloat16), TN, preferred_element_type=jnp.float32
    ).astype(out_ref.dtype)


def mix_tracks(rows, place, norm_gains, time_kernels, mix_up, mix_down, tracks):
    def kernel(*refs):
        mixer_kernel(tracks, *refs)

    return pl.pallas_call(
        kernel,
        out_shape=jax.ShapeDtypeStruct(rows.shape, rows.dtype),
        in_specs=[VMEM] * 4 + [HBM, HBM],
        out_specs=VMEM,
        scratch_shapes=[
            pltpu.VMEM(mix_up.shape, mix_up.dtype),
            pltpu.VMEM(mix_down.shape, mix_down.dtype),
            pltpu.SemaphoreType.DMA((2, mix_up.shape[0], pl.cdiv(mix_up.shape[2], 1024))),
        ],
        compiler_params=pltpu.CompilerParams(vmem_limit_bytes=53 * MIB),
        name="mixer",
    )(rows, place, norm_gains, time_kernels, mix_up, mix_down)


def on_device(
    features,
    query_frame,
    query_pos,
    frame_order,
    conv1_weight,
    conv1_bias,
    conv2_weight,
    proj_weight,
    norm_gains,
    time_kernels,
    mix_up,
    mix_down,
):
    devices = lax.axis_size(AXIS)
    tracks = query_frame.shape[0] // devices
    side = math.isqrt(features.shape[1])
    grid = math.isqrt(proj_weight.shape[0] // conv2_weight.shape[0])

    mine, other = pick_queries(features, query_frame, query_pos)
    ch1, ch2 = conv1_weight.shape[0], conv2_weight.shape[0]
    convs = (conv1_weight, conv1_bias, conv2_weight)
    if devices & (devices - 1):
        even = lax.axis_index(AXIS) % 2 == 0
        half = mine.shape[0]
        both = jnp.concatenate([jnp.where(even, mine, other), jnp.where(even, other, mine)], axis=0)
        both = lax.psum(both, AXIS)
        mine = jnp.where(even, both[:half], both[half:])
        other = jnp.where(even, both[half:], both[:half])
        tables = conv_tables(*convs, side, grid)
        proj = order_proj(proj_weight, ch1, ch2, grid)
    else:
        swap = [(i, i ^ 1) for i in range(devices)]
        mine = mine + lax.ppermute(other, AXIS, swap)
        mine, convs = lax.optimization_barrier((mine, convs))
        tables = conv_tables(*convs, side, grid)
        stages = exchange_stages(devices)
        mine = exchange(mine, stages[0], devices)
        mine, tables, proj_weight = lax.optimization_barrier((mine, tables, proj_weight))
        proj = order_proj(proj_weight, ch1, ch2, grid)
        for shifts in stages[1:]:
            mine = exchange(mine, shifts, devices)
        mine, proj = lax.optimization_barrier((mine, proj))
        other = lax.ppermute(mine, AXIS, swap)
    rows = frame_rows(mine, other, features, tables, proj, side, grid)
    rows = lax.all_to_all(rows, AXIS, split_axis=0, concat_axis=0, tiled=True)
    place = frame_order.reshape(1, -1)
    mixed = mix_tracks(rows, place, norm_gains, time_kernels.transpose(1, 0, 2), mix_up, mix_down, tracks)
    mixed = lax.all_to_all(mixed, AXIS, split_axis=0, concat_axis=0, tiled=True)
    return mixed[None]


def solution(mesh):
    placed = (
        P(("groups", "frames"), None, None),
        P("groups"),
        P("groups"),
        P("groups"),
        P(),
        P(),
        P(),
        P(),
        P(),
        P(),
        P(),
        P(),
    )
    return jax.shard_map(
        on_device,
        mesh=mesh,
        in_specs=placed,
        out_specs=P(("groups", "frames"), None, None),
        check_vma=False,
    )
```
